512 devices in a mesh: frame: 64 (over x, y, core), space: 8 (over z).
Axes of the slice: x: 4, y: 8, z: 8, core: 2. Of those that a mesh axis runs over, the one named last changes fastest.
Arguments:
- queries: bfloat16 [64, 256, 3072], P('frame', 'space'), may hold values from -8 to 8
- keys: bfloat16 [64, 256, 3072], P('frame', 'space'), may hold values from -8 to 8
- values: bfloat16 [64, 256, 3072], P('frame', 'space'), may hold values from -6 to 6
- windows: int32 [64, 8], P('frame'), may hold values from 1 to 16, as said below
Outputs:
- attended: bfloat16 [64, 256, 3072], P('frame', 'space')
The draws below stay inside these ranges and needn't reach their ends.
Inputs may be any that keep to these rules, and one draw needn't show every extreme that they name: `windows`: column 2k and column 2k + 1 lie between max(1, 32 // 2^(k+2)) and 32 // 2^(k+1), and each column reaches its upper end at some frame.
All inputs are finite; a program needn't handle non-finite values.
Results may differ from the reference program's by a relative error of at most 0.006.
Values may be sent and summed in bfloat16 or wider, within the bound.
No kernel may reach another device: no remote copies, remote signals or barrier semaphores. Data moves between devices by JAX's collectives and lax.ppermute only.
A program may use at most 128 MiB of HBM per device.

```python
import math
import jax
import jax.numpy as jnp
from jax import lax

HEADS = 24
HD = 128
OCTAVES = 4
S_DEV = 32
FRAMES = 64
S_ROWS = 256


def draw_queries(key, part):
    key = jax.random.fold_in(key, 11)
    drawn = 1.4 * jax.random.truncated_normal(key, -4.0, 4.0, (FRAMES, S_ROWS, HEADS * HD), jnp.float32)
    return drawn.astype(jnp.bfloat16)


def draw_keys(key, part):
    key = jax.random.fold_in(key, 23)
    drawn = 1.4 * jax.random.truncated_normal(key, -4.0, 4.0, (FRAMES, S_ROWS, HEADS * HD), jnp.float32)
    return drawn.astype(jnp.bfloat16)


def draw_windows(key, part):
    key = jax.random.fold_in(key, 7)
    columns = []
    for octave in range(OCTAVES):
        upper = S_DEV // 2 ** (octave + 1)
        lower = max(upper // 2, 1)
        for side_index in range(2):
            column_key = jax.random.fold_in(key, 2 * octave + side_index)
            first_key, second_key = jax.random.split(column_key)
            widths = jax.random.randint(first_key, (FRAMES,), lower, upper + 1)
            chosen = jax.random.randint(second_key, (), 0, FRAMES)
            widths = jnp.where(jnp.arange(FRAMES) == chosen, upper, widths)
            columns.append(widths)
    return jnp.stack(columns, axis=1).astype(jnp.int32)


def levels(stream_key, extent, cuts, least, high):
    def one(position, blocks):
        heights = jax.random.uniform(jax.random.fold_in(jax.random.fold_in(stream_key, 6), position), (blocks,), jnp.float32, least / len(cuts), high / len(cuts))
        return jnp.repeat(jnp.exp(heights), extent[position] // blocks).reshape((-1,) + (1,) * (len(extent) - position - 1))

    level = one(*cuts[0])
    for cut in cuts[1:]:
        level = level * one(*cut)
    return level


def scatter_about(own_key, shape, scale, reach, cuts=(), kind=jnp.bfloat16):
    values = scale * jax.random.normal(own_key, shape, jnp.float32)
    if cuts:
        values = values * levels(own_key, shape, cuts, -0.22, 0.18)
    return jnp.clip(values, -reach, reach).astype(kind)


def setup_inputs(seed: int = 0) -> dict:
    splits = jax.random.split(jax.random.key(seed), 5)
    return {
        "queries": draw_queries(jax.random.fold_in(splits[4], 71), 0),
        "keys": draw_keys(jax.random.fold_in(splits[4], 71), 0),
        "values": scatter_about(splits[2], (FRAMES, S_ROWS, HEADS * HD), 1.0, 6.0, ((0, 64), (1, 8))),
        "windows": draw_windows(jax.random.fold_in(splits[4], 71), 0),
    }


def attend_frame(frame_idx, queries, keys, values, windows):
    row_index = jnp.arange(S_ROWS)
    query_heads = queries[frame_idx].astype(jnp.float32).reshape(S_ROWS, HEADS, HD)
    key_list = [keys[frame_idx]]
    value_list = [values[frame_idx]]
    mask_list = [jnp.ones((S_ROWS, S_ROWS), dtype=bool)]
    for octave in range(OCTAVES):
        for column, offset in ((2 * octave, -2 ** octave), (2 * octave + 1, 2 ** octave)):
            partner = frame_idx + offset
            inside = (partner >= 0) & (partner < FRAMES)
            clamped = jnp.clip(partner, 0, FRAMES - 1).astype(jnp.int32)
            key_list.append(lax.dynamic_index_in_dim(keys, clamped, 0, keepdims=False))
            value_list.append(lax.dynamic_index_in_dim(values, clamped, 0, keepdims=False))
            half_width = windows[frame_idx, column]
            band = jnp.abs(row_index[:, None] - row_index[None, :]) <= half_width
            mask_list.append(band & inside)
    all_keys = jnp.concatenate(key_list, 0).astype(jnp.float32).reshape(-1, HEADS, HD)
    all_values = jnp.concatenate(value_list, 0).astype(jnp.float32).reshape(-1, HEADS, HD)
    allowed = jnp.concatenate(mask_list, 1)
    scores = jnp.einsum('shd,thd->hst', query_heads, all_keys) * (1.0 / math.sqrt(HD))
    scores = jnp.where(allowed[None], scores, -jnp.inf)
    row_max = lax.optimization_barrier(jnp.max(scores, axis=-1, keepdims=True))
    weights = jnp.exp(scores - row_max)
    denominator = lax.optimization_barrier(jnp.sum(weights, axis=-1))
    rounded = weights.astype(jnp.bfloat16).astype(jnp.float32)
    summed = jnp.einsum('hst,thd->shd', rounded, all_values)
    result = summed / jnp.transpose(denominator)[:, :, None]
    return result.reshape(S_ROWS, HEADS * HD).astype(jnp.bfloat16)

def reference(queries, keys, values, windows):

    def one_frame(frame_idx):
        return attend_frame(frame_idx, queries, keys, values, windows)
    return lax.map(one_frame, jnp.arange(FRAMES, dtype=jnp.int32))
```

```python
import functools
import math

import jax
import jax.numpy as jnp
from jax import lax
from jax.experimental import pallas as pl
from jax.experimental.pallas import tpu as pltpu
from jax.sharding import PartitionSpec as P

HD = 128
OCTAVES = 4
Q_ROWS = 64
K_ROWS = 128

neg_large = -1e30
vmem_bytes = 40 * 1024 * 1024


def crossed(array, by, sense):
    length = lax.axis_size("frame")
    signs = [sense if i % 2 == 0 else -sense for i in range(length)]
    return lax.ppermute(array, "frame", [(i, (i + by * s) % length) for i, s in enumerate(signs)])


def dot_nt(left, right):
    return lax.dot_general(
        left, right, (((1,), (1,)), ((), ())), preferred_element_type=jnp.float32
    )


def dot_nn(left, right):
    return lax.dot_general(
        left, right, (((1,), (0,)), ((), ())), preferred_element_type=jnp.float32
    )


def key_start(block, frame_rows):
    return min(max(block * Q_ROWS - (K_ROWS - Q_ROWS) // 2, 0), frame_rows - K_ROWS)


def rows_of(ref, part, at, start=0, count=None):
    whole = ref[:, part, :, at] if part is not None else ref[:, :, at]
    whole = whole.reshape(whole.shape[0] * whole.shape[1], HD)
    return whole if count is None else whole[start : start + count]


def banded(query_block, block, frame_rows, reach, refs, at, lean, scale):
    start = key_start(block, frame_rows)
    gap = jnp.abs(lean + (block * Q_ROWS - start))
    tiles = []
    for ref, limit in zip(refs, reach):
        keys = rows_of(ref, 0, at, start, K_ROWS)
        tiles.append(jnp.where(gap <= limit, dot_nt(query_block, keys) * scale, neg_large))
    return tiles


def folded(tiles, combine):
    while len(tiles) > 1:
        tiles = [
            combine(*tiles[i : i + 2]) if i + 1 < len(tiles) else tiles[i]
            for i in range(0, len(tiles), 2)
        ]
    return tiles[0]


def row_gap():
    return lax.broadcasted_iota(jnp.int32, (Q_ROWS, K_ROWS), 0) - lax.broadcasted_iota(
        jnp.int32, (Q_ROWS, K_ROWS), 1
    )


def weigh(tiles, top):
    weights = [jnp.exp2(tile - top) for tile in tiles]
    total = jnp.sum(folded(weights, jnp.add), axis=1, keepdims=True)
    return jnp.concatenate([w.astype(jnp.bfloat16) for w in weights], 1), total


def near_kernel(frame_rows, columns, scale, reach, queries, own, *refs):
    partner_refs = refs[: len(columns)]
    top_out, sum_out, product_out = refs[len(columns) :]
    lean = row_gap()
    limits = [reach[column] for column in columns]
    blocks = range(frame_rows // Q_ROWS)
    for head in range(queries.shape[2] // HD):
        at = slice(head * HD, (head + 1) * HD)
        all_queries = rows_of(queries, None, at)
        own_keys = rows_of(own, 0, at)
        own_values = rows_of(own, 1, at)
        for block in blocks:
            rows = slice(block * Q_ROWS, (block + 1) * Q_ROWS)
            query_block = all_queries[rows]
            own_scores = dot_nt(query_block, own_keys) * scale
            tiles = [own_scores[:, k : k + K_ROWS] for k in range(0, frame_rows, K_ROWS)]
            tiles += banded(
                query_block, block, frame_rows, limits, partner_refs, at, lean, scale
            )
            top = jnp.max(folded(tiles, jnp.maximum), axis=1, keepdims=True)
            weights, total = weigh(tiles, top)
            start = key_start(block, frame_rows)
            values = [rows_of(ref, 1, at, start, K_ROWS) for ref in partner_refs]
            top_out[head, rows] = jnp.broadcast_to(top, (Q_ROWS, HD))
            sum_out[head, rows] = jnp.broadcast_to(total, (Q_ROWS, HD))
            product_out[head, rows] = dot_nn(weights, jnp.concatenate([own_values] + values, 0))


def far_kernel(frame_rows, columns, scale, reach, queries, top_in, sum_in, product_in, *refs):
    partner_refs = refs[: len(columns)]
    out = refs[len(columns)]
    lean = row_gap()
    limits = [reach[column] for column in columns]
    parts = Q_ROWS // out.shape[1]
    blocks = range(frame_rows // Q_ROWS)
    span = [slice(block * Q_ROWS, (block + 1) * Q_ROWS) for block in blocks]
    for head in range(queries.shape[2] // HD):
        at = slice(head * HD, (head + 1) * HD)
        all_queries = rows_of(queries, None, at)
        tiles = [
            banded(all_queries[span[b]], b, frame_rows, limits, partner_refs, at, lean, scale)
            for b in blocks
        ]
        tops = [
            jnp.maximum(
                top_in[head, span[b]],
                jnp.max(folded(tiles[b], jnp.maximum), axis=1, keepdims=True),
            )
            for b in blocks
        ]
        weighed = [weigh(tiles[b], tops[b]) for b in blocks]
        products = [
            dot_nn(
                weighed[b][0],
                jnp.concatenate(
                    [
                        rows_of(ref, 1, at, key_start(b, frame_rows), K_ROWS)
                        for ref in partner_refs
                    ],
                    0,
                ),
            )
            for b in blocks
        ]
        for b in blocks:
            shrink = jnp.exp2(top_in[head, span[b]] - tops[b])
            total = sum_in[head, span[b]] * shrink + weighed[b][1]
            product = product_in[head, span[b]] * shrink + products[b]
            out[b * parts : (b + 1) * parts, :, at] = (
                (product / total).astype(jnp.bfloat16).reshape(parts, out.shape[1], HD)
            )


def near_call(reach, queries, own, partners, columns, scale):
    space, rows, feat = queries.shape
    state = jax.ShapeDtypeStruct((feat // HD, space * rows, HD), jnp.float32)
    return pl.pallas_call(
        functools.partial(near_kernel, space * rows, columns, scale),
        in_specs=[pl.BlockSpec(memory_space=pltpu.SMEM)]
        + [pl.BlockSpec(memory_space=pltpu.VMEM)] * (2 + len(columns)),
        out_specs=[pl.BlockSpec(memory_space=pltpu.VMEM)] * 3,
        out_shape=[state] * 3,
        compiler_params=pltpu.CompilerParams(vmem_limit_bytes=vmem_bytes),
        cost_estimate=pl.CostEstimate(
            flops=1_000_000_000, bytes_accessed=6_000_000, transcendentals=1_000_000
        ),
        name="own_and_near",
    )(reach, queries, own, *partners)


def far_call(reach, queries, state, partners, columns, scale):
    space, rows, feat = queries.shape
    return pl.pallas_call(
        functools.partial(far_kernel, space * rows, columns, scale),
        in_specs=[pl.BlockSpec(memory_space=pltpu.SMEM)]
        + [pl.BlockSpec(memory_space=pltpu.VMEM)] * (4 + len(columns)),
        out_specs=pl.BlockSpec(memory_space=pltpu.VMEM),
        out_shape=jax.ShapeDtypeStruct((space, rows, feat), jnp.bfloat16),
        compiler_params=pltpu.CompilerParams(vmem_limit_bytes=vmem_bytes),
        cost_estimate=pl.CostEstimate(
            flops=2_000_000_000, bytes_accessed=4_000_000, transcendentals=500_000
        ),
        name="far_and_merge",
    )(reach, queries, *state, *partners)


def heads_plan(queries, keys, values, windows, scale):
    rows, feat = queries.shape[1:]
    space = lax.axis_size("space")
    frame_pos = lax.axis_index("frame")
    frame_count = lax.axis_size("frame")
    wide = feat // space

    distance = 2 ** jnp.arange(OCTAVES, dtype=jnp.int32)
    below = jnp.where(frame_pos - distance >= 0, windows[0, 0::2], -1)
    above = jnp.where(frame_pos + distance < frame_count, windows[0, 1::2], -1)
    upper = ((frame_pos & 1) == 0) == (distance == 1)
    reach = jnp.concatenate([jnp.where(upper, above, below), jnp.where(upper, below, above)])

    pair = jnp.stack([keys[0], values[0]]).reshape(2, rows, space, wide)
    own = lax.all_to_all(jnp.transpose(pair, (2, 0, 1, 3)), "space", 0, 0, tiled=True)

    split = jnp.transpose(queries[0].reshape(rows, space, wide), (1, 0, 2))
    first_eight = crossed(own, 8, 1)
    first_two = crossed(own, 2, 1)
    second_two = crossed(own, 2, -1)
    first_one = crossed(own, 1, 1)
    split = lax.all_to_all(split, "space", 0, 0, tiled=True)
    first_two, second_two, split = lax.optimization_barrier((first_two, second_two, split))
    first_four = crossed(first_two, 2, 1)
    second_four = crossed(second_two, 2, -1)
    own_late, _ = lax.optimization_barrier((own, first_two))
    second_one = crossed(own_late, 1, -1)
    second_eight = crossed(first_eight, 16, -1)

    near = [first_one, second_one, first_two, second_two]
    state = near_call(reach, split, own, near, [0, 4, 1, 5], scale)
    far = [first_four, second_four, first_eight, second_eight]
    result = far_call(
        reach, split, state, far, [2, 6, 3, 7], scale
    )
    result = lax.all_to_all(result, "space", 0, 0, tiled=True)
    return jnp.transpose(result, (1, 0, 2)).reshape(1, rows, feat)


def shards(queries, keys, values, windows):
    scale = math.log2(math.e) / math.sqrt(HD)
    return heads_plan(queries, keys, values, windows, scale)


def solution(mesh):
    return jax.shard_map(
        shards,
        mesh=mesh,
        in_specs=(
            P("frame", "space", None),
            P("frame", "space", None),
            P("frame", "space", None),
            P("frame", None),
        ),
        out_specs=P("frame", "space", None),
        check_vma=False,
    )
```

```python
import functools
import math

import jax
import jax.numpy as jnp
from jax import lax
from jax.experimental import pallas as pl
from jax.experimental.pallas import tpu as pltpu
from jax.sharding import PartitionSpec as P

HD = 128
OCTAVES = 4
Q_ROWS = 64
K_ROWS = 128

neg_large = -1e30
vmem_bytes = 40 * 1024 * 1024


def crossed(array, by, sense):
    length = lax.axis_size("frame")
    signs = [sense if i % 2 == 0 else -sense for i in range(length)]
    return lax.ppermute(array, "frame", [(i, (i + by * s) % length) for i, s in enumerate(signs)])


def dot_nt(left, right):
    return lax.dot_general(
        left, right, (((1,), (1,)), ((), ())), preferred_element_type=jnp.float32
    )


def dot_nn(left, right):
    return lax.dot_general(
        left, right, (((1,), (0,)), ((), ())), preferred_element_type=jnp.float32
    )


def key_start(block, frame_rows):
    return min(max(block * Q_ROWS - (K_ROWS - Q_ROWS) // 2, 0), frame_rows - K_ROWS)


def rows_of(ref, part, at, start=0, count=None):
    whole = ref[:, part, :, at] if part is not None else ref[:, :, at]
    whole = whole.reshape(whole.shape[0] * whole.shape[1], HD)
    return whole if count is None else whole[start : start + count]


def banded(query_block, block, frame_rows, reach, refs, at, lean, scale):
    start = key_start(block, frame_rows)
    gap = jnp.abs(lean + (block * Q_ROWS - start))
    tiles = []
    for ref, limit in zip(refs, reach):
        keys = rows_of(ref, 0, at, start, K_ROWS)
        tiles.append(jnp.where(gap <= limit, dot_nt(query_block, keys) * scale, neg_large))
    return tiles


def folded(tiles, combine):
    while len(tiles) > 1:
        tiles = [
            combine(*tiles[i : i + 2]) if i + 1 < len(tiles) else tiles[i]
            for i in range(0, len(tiles), 2)
        ]
    return tiles[0]


def row_gap():
    return lax.broadcasted_iota(jnp.int32, (Q_ROWS, K_ROWS), 0) - lax.broadcasted_iota(
        jnp.int32, (Q_ROWS, K_ROWS), 1
    )


def weigh(tiles, top):
    weights = [jnp.exp2(tile - top) for tile in tiles]
    total = jnp.sum(folded(weights, jnp.add), axis=1, keepdims=True)
    return jnp.concatenate([w.astype(jnp.bfloat16) for w in weights], 1), total


def near_kernel(frame_rows, columns, scale, reach, queries, own, *refs):
    partner_refs = refs[: len(columns)]
    top_out, sum_out, product_out = refs[len(columns) :]
    lean = row_gap()
    limits = [reach[column] for column in columns]
    blocks = range(frame_rows // Q_ROWS)
    for head in range(queries.shape[2] // HD):
        at = slice(head * HD, (head + 1) * HD)
        all_queries = rows_of(queries, None, at)
        own_keys = rows_of(own, 0, at)
        own_values = rows_of(own, 1, at)
        for block in blocks:
            rows = slice(block * Q_ROWS, (block + 1) * Q_ROWS)
            query_block = all_queries[rows]
            own_scores = dot_nt(query_block, own_keys) * scale
            tiles = [own_scores[:, k : k + K_ROWS] for k in range(0, frame_rows, K_ROWS)]
            tiles += banded(
                query_block, block, frame_rows, limits, partner_refs, at, lean, scale
            )
            top = jnp.max(folded(tiles, jnp.maximum), axis=1, keepdims=True)
            weights, total = weigh(tiles, top)
            start = key_start(block, frame_rows)
            values = [rows_of(ref, 1, at, start, K_ROWS) for ref in partner_refs]
            top_out[head, rows] = jnp.broadcast_to(top, (Q_ROWS, HD))
            sum_out[head, rows] = jnp.broadcast_to(total, (Q_ROWS, HD))
            product_out[head, rows] = dot_nn(weights, jnp.concatenate([own_values] + values, 0))


def far_kernel(frame_rows, columns, scale, reach, queries, top_in, sum_in, product_in, *refs):
    partner_refs = refs[: len(columns)]
    out = refs[len(columns)]
    lean = row_gap()
    limits = [reach[column] for column in columns]
    parts = Q_ROWS // out.shape[1]
    blocks = range(frame_rows // Q_ROWS)
    span = [slice(block * Q_ROWS, (block + 1) * Q_ROWS) for block in blocks]
    for head in range(queries.shape[2] // HD):
        at = slice(head * HD, (head + 1) * HD)
        all_queries = rows_of(queries, None, at)
        tiles = [
            banded(all_queries[span[b]], b, frame_rows, limits, partner_refs, at, lean, scale)
            for b in blocks
        ]
        tops = [
            jnp.maximum(
                top_in[head, span[b]],
                jnp.max(folded(tiles[b], jnp.maximum), axis=1, keepdims=True),
            )
            for b in blocks
        ]
        weighed = [weigh(tiles[b], tops[b]) for b in blocks]
        products = [
            dot_nn(
                weighed[b][0],
                jnp.concatenate(
                    [
                        rows_of(ref, 1, at, key_start(b, frame_rows), K_ROWS)
                        for ref in partner_refs
                    ],
                    0,
                ),
            )
            for b in blocks
        ]
        for b in blocks:
            shrink = jnp.exp2(top_in[head, span[b]] - tops[b])
            total = sum_in[head, span[b]] * shrink + weighed[b][1]
            product = product_in[head, span[b]] * shrink + products[b]
            out[b * parts : (b + 1) * parts, :, at] = (
                (product / total).astype(jnp.bfloat16).reshape(parts, out.shape[1], HD)
            )


def near_call(reach, queries, own, partners, columns, scale):
    space, rows, feat = queries.shape
    state = jax.ShapeDtypeStruct((feat // HD, space * rows, HD), jnp.float32)
    return pl.pallas_call(
        functools.partial(near_kernel, space * rows, columns, scale),
        in_specs=[pl.BlockSpec(memory_space=pltpu.SMEM)]
        + [pl.BlockSpec(memory_space=pltpu.VMEM)] * (2 + len(columns)),
        out_specs=[pl.BlockSpec(memory_space=pltpu.VMEM)] * 3,
        out_shape=[state] * 3,
        compiler_params=pltpu.CompilerParams(vmem_limit_bytes=vmem_bytes),
        cost_estimate=pl.CostEstimate(
            flops=1_000_000_000, bytes_accessed=6_000_000, transcendentals=1_000_000
        ),
        name="own_and_near",
    )(reach, queries, own, *partners)


def far_call(reach, queries, state, partners, columns, scale):
    space, rows, feat = queries.shape
    return pl.pallas_call(
        functools.partial(far_kernel, space * rows, columns, scale),
        in_specs=[pl.BlockSpec(memory_space=pltpu.SMEM)]
        + [pl.BlockSpec(memory_space=pltpu.VMEM)] * (4 + len(columns)),
        out_specs=pl.BlockSpec(memory_space=pltpu.VMEM),
        out_shape=jax.ShapeDtypeStruct((space, rows, feat), jnp.bfloat16),
        compiler_params=pltpu.CompilerParams(vmem_limit_bytes=vmem_bytes),
        cost_estimate=pl.CostEstimate(
            flops=2_000_000_000, bytes_accessed=4_000_000, transcendentals=500_000
        ),
        name="far_and_merge",
    )(reach, queries, *state, *partners)


def heads_plan(queries, keys, values, windows, scale):
    rows, feat = queries.shape[1:]
    space = lax.axis_size("space")
    frame_pos = lax.axis_index("frame")
    frame_count = lax.axis_size("frame")
    wide = feat // space

    distance = 2 ** jnp.arange(OCTAVES, dtype=jnp.int32)
    below = jnp.where(frame_pos - distance >= 0, windows[0, 0::2], -1)
    above = jnp.where(frame_pos + distance < frame_count, windows[0, 1::2], -1)
    upper = ((frame_pos & 1) == 0) == (distance == 1)
    reach = jnp.concatenate([jnp.where(upper, above, below), jnp.where(upper, below, above)])

    pair = jnp.stack([keys[0], values[0]]).reshape(2, rows, space, wide)
    own = lax.all_to_all(jnp.transpose(pair, (2, 0, 1, 3)), "space", 0, 0, tiled=True)

    split = jnp.transpose(queries[0].reshape(rows, space, wide), (1, 0, 2))
    first_eight = crossed(own, 8, 1)
    first_one = crossed(own, 1, 1)
    first_two = crossed(own, 2, 1)
    second_one = crossed(first_one, 2, 1)
    second_two = crossed(second_one, 1, 1)
    first_four = crossed(first_two, 2, 1)
    three = crossed(second_one, 2, 1)
    second_four = crossed(three, 1, 1)
    split, _ = lax.optimization_barrier((split, first_two))
    split = lax.all_to_all(split, "space", 0, 0, tiled=True)
    first_eight, split = lax.optimization_barrier((first_eight, split))
    second_eight = crossed(first_eight, 16, -1)

    near = [first_one, second_one, first_two, first_four]
    state = near_call(reach, split, own, near, [0, 4, 1, 2], scale)
    far = [second_two, second_four, first_eight, second_eight]
    result = far_call(reach, split, state, far, [5, 6, 3, 7], scale)
    result = lax.all_to_all(result, "space", 0, 0, tiled=True)
    return jnp.transpose(result, (1, 0, 2)).reshape(1, rows, feat)


def shards(queries, keys, values, windows):
    scale = math.log2(math.e) / math.sqrt(HD)
    return heads_plan(queries, keys, values, windows, scale)


def solution(mesh):
    return jax.shard_map(
        shards,
        mesh=mesh,
        in_specs=(
            P("frame", "space", None),
            P("frame", "space", None),
            P("frame", "space", None),
            P("frame", None),
        ),
        out_specs=P("frame", "space", None),
        check_vma=False,
    )
```

```python
import functools
import math

import jax
import jax.numpy as jnp
from jax import lax
from jax.experimental import pallas as pl
from jax.experimental.pallas import tpu as pltpu
from jax.sharding import PartitionSpec as P

HD = 128
OCTAVES = 4
Q_ROWS = 64
K_ROWS = 128

neg_large = -1e30
vmem_bytes = 40 * 1024 * 1024


def crossed(array, by, sense):
    length = lax.axis_size("frame")
    signs = [sense if i % 2 == 0 else -sense for i in range(length)]
    return lax.ppermute(array, "frame", [(i, (i + by * s) % length) for i, s in enumerate(signs)])


def dot_nt(left, right):
    return lax.dot_general(
        left, right, (((1,), (1,)), ((), ())), preferred_element_type=jnp.float32
    )


def dot_nn(left, right):
    return lax.dot_general(
        left, right, (((1,), (0,)), ((), ())), preferred_element_type=jnp.float32
    )


def key_start(block, frame_rows):
    return min(max(block * Q_ROWS - (K_ROWS - Q_ROWS) // 2, 0), frame_rows - K_ROWS)


def rows_of(ref, part, at, start=0, count=None):
    whole = ref[:, part, :, at]
    whole = whole.reshape(whole.shape[0] * whole.shape[1], HD)
    return whole if count is None else whole[start : start + count]


def banded(query_block, block, frame_rows, reach, refs, at, lean, scale):
    start = key_start(block, frame_rows)
    gap = jnp.abs(lean + (block * Q_ROWS - start))
    tiles = []
    for ref, limit in zip(refs, reach):
        keys = rows_of(ref, 0, at, start, K_ROWS)
        tiles.append(jnp.where(gap <= limit, dot_nt(query_block, keys) * scale, neg_large))
    return tiles


def folded(tiles, combine):
    while len(tiles) > 1:
        tiles = [
            combine(*tiles[i : i + 2]) if i + 1 < len(tiles) else tiles[i]
            for i in range(0, len(tiles), 2)
        ]
    return tiles[0]


def row_gap():
    return lax.broadcasted_iota(jnp.int32, (Q_ROWS, K_ROWS), 0) - lax.broadcasted_iota(
        jnp.int32, (Q_ROWS, K_ROWS), 1
    )


def weigh(tiles, top):
    weights = [jnp.exp2(tile - top) for tile in tiles]
    total = jnp.sum(folded(weights, jnp.add), axis=1, keepdims=True)
    return jnp.concatenate([w.astype(jnp.bfloat16) for w in weights], 1), total


def split_kernel(pair, queries, out):
    wide = out.shape[-1]
    for share in range(out.shape[0]):
        at = slice(share * wide, (share + 1) * wide)
        out[share, 0] = pair[0, :, at]
        out[share, 1] = pair[1, :, at]
        out[share, 2] = queries[0, :, at]


def split_call(pair, queries, space):
    _, rows, feat = pair.shape
    return pl.pallas_call(
        split_kernel,
        in_specs=[pl.BlockSpec(memory_space=pltpu.VMEM)] * 2,
        out_specs=pl.BlockSpec(memory_space=pltpu.VMEM),
        out_shape=jax.ShapeDtypeStruct((space, 3, rows, feat // space), pair.dtype),
        compiler_params=pltpu.CompilerParams(vmem_limit_bytes=vmem_bytes),
        cost_estimate=pl.CostEstimate(
            flops=20_000_000_000, bytes_accessed=1_200_000, transcendentals=0
        ),
        name="heads_apart",
    )(pair, queries)


def near_kernel(frame_rows, columns, scale, reach, queries, own, *refs):
    partner_refs = refs[: len(columns)]
    top_out, sum_out, product_out = refs[len(columns) :]
    lean = row_gap()
    limits = [reach[column] for column in columns]
    blocks = range(frame_rows // Q_ROWS)
    for head in range(own.shape[3] // HD):
        at = slice(head * HD, (head + 1) * HD)
        all_queries = rows_of(queries, 2, at)
        own_keys = rows_of(own, 0, at)
        own_values = rows_of(own, 1, at)
        for block in blocks:
            rows = slice(block * Q_ROWS, (block + 1) * Q_ROWS)
            query_block = all_queries[rows]
            own_scores = dot_nt(query_block, own_keys) * scale
            tiles = [own_scores[:, k : k + K_ROWS] for k in range(0, frame_rows, K_ROWS)]
            tiles += banded(
                query_block, block, frame_rows, limits, partner_refs, at, lean, scale
            )
            top = jnp.max(folded(tiles, jnp.maximum), axis=1, keepdims=True)
            weights, total = weigh(tiles, top)
            start = key_start(block, frame_rows)
            values = [rows_of(ref, 1, at, start, K_ROWS) for ref in partner_refs]
            top_out[head, rows] = jnp.broadcast_to(top, (Q_ROWS, HD))
            sum_out[head, rows] = jnp.broadcast_to(total, (Q_ROWS, HD))
            product_out[head, rows] = dot_nn(weights, jnp.concatenate([own_values] + values, 0))


def far_kernel(frame_rows, columns, scale, reach, queries, top_in, sum_in, product_in, *refs):
    partner_refs = refs[: len(columns)]
    out = refs[len(columns)]
    lean = row_gap()
    limits = [reach[column] for column in columns]
    parts = Q_ROWS // out.shape[1]
    blocks = range(frame_rows // Q_ROWS)
    span = [slice(block * Q_ROWS, (block + 1) * Q_ROWS) for block in blocks]
    for head in range(queries.shape[3] // HD):
        at = slice(head * HD, (head + 1) * HD)
        all_queries = rows_of(queries, 2, at)
        tiles = [
            banded(all_queries[span[b]], b, frame_rows, limits, partner_refs, at, lean, scale)
            for b in blocks
        ]
        tops = [
            jnp.maximum(
                top_in[head, span[b]],
                jnp.max(folded(tiles[b], jnp.maximum), axis=1, keepdims=True),
            )
            for b in blocks
        ]
        weighed = [weigh(tiles[b], tops[b]) for b in blocks]
        products = [
            dot_nn(
                weighed[b][0],
                jnp.concatenate(
                    [
                        rows_of(ref, 1, at, key_start(b, frame_rows), K_ROWS)
                        for ref in partner_refs
                    ],
                    0,
                ),
            )
            for b in blocks
        ]
        for b in blocks:
            shrink = jnp.exp2(top_in[head, span[b]] - tops[b])
            total = sum_in[head, span[b]] * shrink + weighed[b][1]
            product = product_in[head, span[b]] * shrink + products[b]
            out[b * parts : (b + 1) * parts, :, at] = (
                (product / total).astype(jnp.bfloat16).reshape(parts, out.shape[1], HD)
            )


def near_call(reach, queries, own, partners, columns, scale):
    space, _, rows, feat = own.shape
    state = jax.ShapeDtypeStruct((feat // HD, space * rows, HD), jnp.float32)
    return pl.pallas_call(
        functools.partial(near_kernel, space * rows, columns, scale),
        in_specs=[pl.BlockSpec(memory_space=pltpu.SMEM)]
        + [pl.BlockSpec(memory_space=pltpu.VMEM)] * (2 + len(columns)),
        out_specs=[pl.BlockSpec(memory_space=pltpu.VMEM)] * 3,
        out_shape=[state] * 3,
        compiler_params=pltpu.CompilerParams(vmem_limit_bytes=vmem_bytes),
        cost_estimate=pl.CostEstimate(
            flops=1_000_000_000, bytes_accessed=6_000_000, transcendentals=1_000_000
        ),
        name="own_and_near",
    )(reach, queries, own, *partners)


def far_call(reach, queries, state, partners, columns, scale):
    space, _, rows, feat = queries.shape
    return pl.pallas_call(
        functools.partial(far_kernel, space * rows, columns, scale),
        in_specs=[pl.BlockSpec(memory_space=pltpu.SMEM)]
        + [pl.BlockSpec(memory_space=pltpu.VMEM)] * (4 + len(columns)),
        out_specs=pl.BlockSpec(memory_space=pltpu.VMEM),
        out_shape=jax.ShapeDtypeStruct((space, rows, feat), jnp.bfloat16),
        compiler_params=pltpu.CompilerParams(vmem_limit_bytes=vmem_bytes),
        cost_estimate=pl.CostEstimate(
            flops=2_000_000_000, bytes_accessed=4_000_000, transcendentals=500_000
        ),
        name="far_and_merge",
    )(reach, queries, *state, *partners)


def heads_plan(queries, keys, values, windows, scale):
    rows, feat = queries.shape[1:]
    space = lax.axis_size("space")
    frame_pos = lax.axis_index("frame")
    frame_count = lax.axis_size("frame")

    distance = 2 ** jnp.arange(OCTAVES, dtype=jnp.int32)
    below = jnp.where(frame_pos - distance >= 0, windows[0, 0::2], -1)
    above = jnp.where(frame_pos + distance < frame_count, windows[0, 1::2], -1)
    upper = ((frame_pos & 1) == 0) == (distance == 1)
    reach = jnp.concatenate([jnp.where(upper, above, below), jnp.where(upper, below, above)])

    pair = jnp.concatenate([keys, values], 0)
    far_rows = crossed(pair, 8, 1)
    shares = jnp.transpose(pair.reshape(2, rows, space, feat // space), (2, 0, 1, 3))
    own = lax.all_to_all(shares, "space", 0, 0, tiled=True)

    first_two = crossed(own, 2, 1)
    second_two = crossed(own, 2, -1)
    first_two, second_two, whole = lax.optimization_barrier(
        (first_two, second_two, split_call(far_rows, queries, space))
    )
    whole = lax.all_to_all(whole, "space", 0, 0, tiled=True)
    first_four = crossed(first_two, 2, 1)
    second_four = crossed(second_two, 2, -1)
    second_eight = crossed(whole[:, :2], 16, -1)
    own_late, _ = lax.optimization_barrier((own, (first_two, second_two)))
    first_one = crossed(own_late, 1, 1)
    second_one = crossed(own_late, 1, -1)

    near = [first_two, second_two, first_four, second_four]
    state = near_call(reach, whole, own, near, [1, 5, 2, 6], scale)
    far = [first_one, second_one, whole, second_eight]
    result = far_call(reach, whole, state, far, [0, 4, 3, 7], scale)
    result = lax.all_to_all(result, "space", 0, 0, tiled=True)
    return jnp.transpose(result, (1, 0, 2)).reshape(1, rows, feat)


def shards(queries, keys, values, windows):
    scale = math.log2(math.e) / math.sqrt(HD)
    return heads_plan(queries, keys, values, windows, scale)


def solution(mesh):
    return jax.shard_map(
        shards,
        mesh=mesh,
        in_specs=(
            P("frame", "space", None),
            P("frame", "space", None),
            P("frame", "space", None),
            P("frame", None),
        ),
        out_specs=P("frame", "space", None),
        check_vma=False,
    )
```

```python
import functools
import math

import jax
import jax.numpy as jnp
from jax import lax
from jax.experimental import pallas as pl
from jax.experimental.pallas import tpu as pltpu
from jax.sharding import PartitionSpec as P

HD = 128
OCTAVES = 4
Q_ROWS = 64
K_ROWS = 128

neg_large = -1e30
vmem_bytes = 40 * 1024 * 1024


def crossed(array, by, sense, keep=None):
    length = lax.axis_size("frame")
    pairs = []
    for frame in range(length):
        target = frame + by * (sense if frame % 2 == 0 else -sense)
        if keep is None and 0 <= target < length:
            pairs.append((frame, target))
        elif keep is not None and keep(target % length, length):
            pairs.append((frame, target % length))
    return lax.ppermute(array, "frame", pairs)


def has_other_far(frame, length):
    return frame + 8 < length if frame % 2 == 0 else frame >= 8


def dot_nt(left, right):
    return lax.dot_general(
        left, right, (((1,), (1,)), ((), ())), preferred_element_type=jnp.float32
    )


def dot_nn(left, right):
    return lax.dot_general(
        left, right, (((1,), (0,)), ((), ())), preferred_element_type=jnp.float32
    )


def key_start(block, frame_rows):
    return min(max(block * Q_ROWS - (K_ROWS - Q_ROWS) // 2, 0), frame_rows - K_ROWS)


def rows_of(ref, part, at, start=0, count=None):
    whole = ref[:, part, :, at] if part is not None else ref[:, :, at]
    whole = whole.reshape(whole.shape[0] * whole.shape[1], HD)
    return whole if count is None else whole[start : start + count]


def banded(query_block, block, frame_rows, reach, refs, at, lean, scale):
    start = key_start(block, frame_rows)
    gap = jnp.abs(lean + (block * Q_ROWS - start))
    tiles = []
    for ref, limit in zip(refs, reach):
        keys = rows_of(ref, 0, at, start, K_ROWS)
        tiles.append(jnp.where(gap <= limit, dot_nt(query_block, keys) * scale, neg_large))
    return tiles


def folded(tiles, combine):
    while len(tiles) > 1:
        tiles = [
            combine(*tiles[i : i + 2]) if i + 1 < len(tiles) else tiles[i]
            for i in range(0, len(tiles), 2)
        ]
    return tiles[0]


def row_gap():
    return lax.broadcasted_iota(jnp.int32, (Q_ROWS, K_ROWS), 0) - lax.broadcasted_iota(
        jnp.int32, (Q_ROWS, K_ROWS), 1
    )


def weigh(tiles, top):
    weights = [jnp.exp2(tile - top) for tile in tiles]
    total = jnp.sum(folded(weights, jnp.add), axis=1, keepdims=True)
    return jnp.concatenate([w.astype(jnp.bfloat16) for w in weights], 1), total


def near_kernel(frame_rows, columns, scale, reach, queries, own, *refs):
    partner_refs = refs[: len(columns)]
    top_out, sum_out, product_out = refs[len(columns) :]
    lean = row_gap()
    limits = [reach[column] for column in columns]
    blocks = range(frame_rows // Q_ROWS)
    for head in range(queries.shape[2] // HD):
        at = slice(head * HD, (head + 1) * HD)
        all_queries = rows_of(queries, None, at)
        own_keys = rows_of(own, 0, at)
        own_values = rows_of(own, 1, at)
        for block in blocks:
            rows = slice(block * Q_ROWS, (block + 1) * Q_ROWS)
            query_block = all_queries[rows]
            own_scores = dot_nt(query_block, own_keys) * scale
            tiles = [own_scores[:, k : k + K_ROWS] for k in range(0, frame_rows, K_ROWS)]
            tiles += banded(
                query_block, block, frame_rows, limits, partner_refs, at, lean, scale
            )
            top = jnp.max(folded(tiles, jnp.maximum), axis=1, keepdims=True)
            weights, total = weigh(tiles, top)
            start = key_start(block, frame_rows)
            values = [rows_of(ref, 1, at, start, K_ROWS) for ref in partner_refs]
            top_out[head, rows] = jnp.broadcast_to(top, (Q_ROWS, HD))
            sum_out[head, rows] = jnp.broadcast_to(total, (Q_ROWS, HD))
            product_out[head, rows] = dot_nn(weights, jnp.concatenate([own_values] + values, 0))


def far_kernel(frame_rows, columns, scale, reach, queries, top_in, sum_in, product_in, *refs):
    partner_refs = refs[: len(columns)]
    out = refs[len(columns)]
    lean = row_gap()
    limits = [reach[column] for column in columns]
    parts = Q_ROWS // out.shape[1]
    blocks = range(frame_rows // Q_ROWS)
    span = [slice(block * Q_ROWS, (block + 1) * Q_ROWS) for block in blocks]
    for head in range(queries.shape[2] // HD):
        at = slice(head * HD, (head + 1) * HD)
        all_queries = rows_of(queries, None, at)
        tiles = [
            banded(all_queries[span[b]], b, frame_rows, limits, partner_refs, at, lean, scale)
            for b in blocks
        ]
        tops = [
            jnp.maximum(
                top_in[head, span[b]],
                jnp.max(folded(tiles[b], jnp.maximum), axis=1, keepdims=True),
            )
            for b in blocks
        ]
        weighed = [weigh(tiles[b], tops[b]) for b in blocks]
        products = [
            dot_nn(
                weighed[b][0],
                jnp.concatenate(
                    [
                        rows_of(ref, 1, at, key_start(b, frame_rows), K_ROWS)
                        for ref in partner_refs
                    ],
                    0,
                ),
            )
            for b in blocks
        ]
        for b in blocks:
            shrink = jnp.exp2(top_in[head, span[b]] - tops[b])
            total = sum_in[head, span[b]] * shrink + weighed[b][1]
            product = product_in[head, span[b]] * shrink + products[b]
            out[b * parts : (b + 1) * parts, :, at] = (
                (product / total).astype(jnp.bfloat16).reshape(parts, out.shape[1], HD)
            )


def near_call(reach, queries, own, partners, columns, scale):
    space, rows, feat = queries.shape
    state = jax.ShapeDtypeStruct((feat // HD, space * rows, HD), jnp.float32)
    return pl.pallas_call(
        functools.partial(near_kernel, space * rows, columns, scale),
        in_specs=[pl.BlockSpec(memory_space=pltpu.SMEM)]
        + [pl.BlockSpec(memory_space=pltpu.VMEM)] * (2 + len(columns)),
        out_specs=[pl.BlockSpec(memory_space=pltpu.VMEM)] * 3,
        out_shape=[state] * 3,
        compiler_params=pltpu.CompilerParams(vmem_limit_bytes=vmem_bytes),
        cost_estimate=pl.CostEstimate(
            flops=1_000_000_000, bytes_accessed=6_000_000, transcendentals=1_000_000
        ),
        name="own_and_near",
    )(reach, queries, own, *partners)


def far_call(reach, queries, state, partners, columns, scale):
    space, rows, feat = queries.shape
    return pl.pallas_call(
        functools.partial(far_kernel, space * rows, columns, scale),
        in_specs=[pl.BlockSpec(memory_space=pltpu.SMEM)]
        + [pl.BlockSpec(memory_space=pltpu.VMEM)] * (4 + len(columns)),
        out_specs=pl.BlockSpec(memory_space=pltpu.VMEM),
        out_shape=jax.ShapeDtypeStruct((space, rows, feat), jnp.bfloat16),
        compiler_params=pltpu.CompilerParams(vmem_limit_bytes=vmem_bytes),
        cost_estimate=pl.CostEstimate(
            flops=2_000_000_000, bytes_accessed=4_000_000, transcendentals=500_000
        ),
        name="far_and_merge",
    )(reach, queries, *state, *partners)


def heads_plan(queries, keys, values, windows, scale):
    rows, feat = queries.shape[1:]
    space = lax.axis_size("space")
    frame_pos = lax.axis_index("frame")
    frame_count = lax.axis_size("frame")
    wide = feat // space

    distance = 2 ** jnp.arange(OCTAVES, dtype=jnp.int32)
    below = jnp.where(frame_pos - distance >= 0, windows[0, 0::2], -1)
    above = jnp.where(frame_pos + distance < frame_count, windows[0, 1::2], -1)
    upper = ((frame_pos & 1) == 0) == (distance == 1)
    reach = jnp.concatenate([jnp.where(upper, above, below), jnp.where(upper, below, above)])

    pair = jnp.stack([keys[0], values[0]]).reshape(2, rows, space, wide)
    own = lax.all_to_all(jnp.transpose(pair, (2, 0, 1, 3)), "space", 0, 0, tiled=True)

    split = jnp.transpose(queries[0].reshape(rows, space, wide), (1, 0, 2))
    first_eight = crossed(own, 8, 1, lambda frame, length: True)
    first_two = crossed(own, 2, 1)
    second_two = crossed(own, 2, -1)
    first_one = crossed(own, 1, 1)
    split = lax.all_to_all(split, "space", 0, 0, tiled=True)
    first_two, second_two, split = lax.optimization_barrier((first_two, second_two, split))
    first_four = crossed(first_two, 2, 1)
    second_four = crossed(second_two, 2, -1)
    own_late, _ = lax.optimization_barrier((own, first_two))
    second_one = crossed(own_late, 1, -1)
    second_eight = crossed(first_eight, 16, -1, has_other_far)

    near = [first_one, second_one, first_two, second_two]
    state = near_call(reach, split, own, near, [0, 4, 1, 5], scale)
    far = [first_four, second_four, first_eight, second_eight]
    result = far_call(
        reach, split, state, far, [2, 6, 3, 7], scale
    )
    result = lax.all_to_all(result, "space", 0, 0, tiled=True)
    return jnp.transpose(result, (1, 0, 2)).reshape(1, rows, feat)


def shards(queries, keys, values, windows):
    scale = math.log2(math.e) / math.sqrt(HD)
    return heads_plan(queries, keys, values, windows, scale)


def solution(mesh):
    return jax.shard_map(
        shards,
        mesh=mesh,
        in_specs=(
            P("frame", "space", None),
            P("frame", "space", None),
            P("frame", "space", None),
            P("frame", None),
        ),
        out_specs=P("frame", "space", None),
        check_vma=False,
    )
```

```python
import functools
import math

import jax
import jax.numpy as jnp
from jax import lax
from jax.experimental import pallas as pl
from jax.experimental.pallas import tpu as pltpu
from jax.sharding import PartitionSpec as P

HD = 128
OCTAVES = 4
Q_ROWS = 64
K_ROWS = 128

neg_large = -1e30
vmem_bytes = 40 * 1024 * 1024


def crossed(array, by, sense, keep=None):
    length = lax.axis_size("frame")
    pairs = []
    for frame in range(length):
        target = frame + by * (sense if frame % 2 == 0 else -sense)
        if keep is None and 0 <= target < length:
            pairs.append((frame, target))
        elif keep is not None and keep(target % length, length):
            pairs.append((frame, target % length))
    return lax.ppermute(array, "frame", pairs)


def has_other_far(frame, length):
    return frame + 8 < length if frame % 2 == 0 else frame >= 8


def dot_nt(left, right):
    return lax.dot_general(
        left, right, (((1,), (1,)), ((), ())), preferred_element_type=jnp.float32
    )


def dot_nn(left, right):
    return lax.dot_general(
        left, right, (((1,), (0,)), ((), ())), preferred_element_type=jnp.float32
    )


def key_start(block, frame_rows):
    return min(max(block * Q_ROWS - (K_ROWS - Q_ROWS) // 2, 0), frame_rows - K_ROWS)


def rows_of(ref, part, at, start=0, count=None):
    whole = ref[:, part, :, at] if part is not None else ref[:, :, at]
    whole = whole.reshape(whole.shape[0] * whole.shape[1], HD)
    return whole if count is None else whole[start : start + count]


def banded(query_block, block, frame_rows, reach, refs, at, lean, scale):
    start = key_start(block, frame_rows)
    gap = jnp.abs(lean + (block * Q_ROWS - start))
    tiles = []
    for ref, limit in zip(refs, reach):
        keys = rows_of(ref, 0, at, start, K_ROWS)
        tiles.append(jnp.where(gap <= limit, dot_nt(query_block, keys) * scale, neg_large))
    return tiles


def folded(tiles, combine):
    while len(tiles) > 1:
        tiles = [
            combine(*tiles[i : i + 2]) if i + 1 < len(tiles) else tiles[i]
            for i in range(0, len(tiles), 2)
        ]
    return tiles[0]


def row_gap():
    return lax.broadcasted_iota(jnp.int32, (Q_ROWS, K_ROWS), 0) - lax.broadcasted_iota(
        jnp.int32, (Q_ROWS, K_ROWS), 1
    )


def weigh(tiles, top):
    weights = [jnp.exp2(tile - top) for tile in tiles]
    total = jnp.sum(folded(weights, jnp.add), axis=1, keepdims=True)
    return jnp.concatenate([w.astype(jnp.bfloat16) for w in weights], 1), total


def near_kernel(frame_rows, columns, scale, reach, queries, own, *refs):
    partner_refs = refs[: len(columns)]
    top_out, sum_out, product_out = refs[len(columns) :]
    lean = row_gap()
    limits = [reach[column] for column in columns]
    blocks = range(frame_rows // Q_ROWS)
    for head in range(queries.shape[2] // HD):
        at = slice(head * HD, (head + 1) * HD)
        all_queries = rows_of(queries, None, at)
        own_keys = rows_of(own, 0, at)
        own_values = rows_of(own, 1, at)
        for block in blocks:
            rows = slice(block * Q_ROWS, (block + 1) * Q_ROWS)
            query_block = all_queries[rows]
            own_scores = dot_nt(query_block, own_keys) * scale
            tiles = [own_scores[:, k : k + K_ROWS] for k in range(0, frame_rows, K_ROWS)]
            tiles += banded(
                query_block, block, frame_rows, limits, partner_refs, at, lean, scale
            )
            top = jnp.max(folded(tiles, jnp.maximum), axis=1, keepdims=True)
            weights, total = weigh(tiles, top)
            start = key_start(block, frame_rows)
            values = [rows_of(ref, 1, at, start, K_ROWS) for ref in partner_refs]
            top_out[head, rows] = jnp.broadcast_to(top, (Q_ROWS, HD))
            sum_out[head, rows] = jnp.broadcast_to(total, (Q_ROWS, HD))
            product_out[head, rows] = dot_nn(weights, jnp.concatenate([own_values] + values, 0))


def far_kernel(frame_rows, columns, scale, reach, queries, top_in, sum_in, product_in, *refs):
    partner_refs = refs[: len(columns)]
    out = refs[len(columns)]
    lean = row_gap()
    limits = [reach[column] for column in columns]
    parts = Q_ROWS // out.shape[1]
    blocks = range(frame_rows // Q_ROWS)
    span = [slice(block * Q_ROWS, (block + 1) * Q_ROWS) for block in blocks]
    for head in range(queries.shape[2] // HD):
        at = slice(head * HD, (head + 1) * HD)
        all_queries = rows_of(queries, None, at)
        tiles = [
            banded(all_queries[span[b]], b, frame_rows, limits, partner_refs, at, lean, scale)
            for b in blocks
        ]
        tops = [
            jnp.maximum(
                top_in[head, span[b]],
                jnp.max(folded(tiles[b], jnp.maximum), axis=1, keepdims=True),
            )
            for b in blocks
        ]
        weighed = [weigh(tiles[b], tops[b]) for b in blocks]
        products = [
            dot_nn(
                weighed[b][0],
                jnp.concatenate(
                    [
                        rows_of(ref, 1, at, key_start(b, frame_rows), K_ROWS)
                        for ref in partner_refs
                    ],
                    0,
                ),
            )
            for b in blocks
        ]
        for b in blocks:
            shrink = jnp.exp2(top_in[head, span[b]] - tops[b])
            total = sum_in[head, span[b]] * shrink + weighed[b][1]
            product = product_in[head, span[b]] * shrink + products[b]
            out[b * parts : (b + 1) * parts, :, at] = (
                (product / total).astype(jnp.bfloat16).reshape(parts, out.shape[1], HD)
            )


def near_call(reach, queries, own, partners, columns, scale):
    space, rows, feat = queries.shape
    state = jax.ShapeDtypeStruct((feat // HD, space * rows, HD), jnp.float32)
    return pl.pallas_call(
        functools.partial(near_kernel, space * rows, columns, scale),
        in_specs=[pl.BlockSpec(memory_space=pltpu.SMEM)]
        + [pl.BlockSpec(memory_space=pltpu.VMEM)] * (2 + len(columns)),
        out_specs=[pl.BlockSpec(memory_space=pltpu.VMEM)] * 3,
        out_shape=[state] * 3,
        compiler_params=pltpu.CompilerParams(vmem_limit_bytes=vmem_bytes),
        cost_estimate=pl.CostEstimate(
            flops=1_000_000_000, bytes_accessed=6_000_000, transcendentals=1_000_000
        ),
        name="own_and_near",
    )(reach, queries, own, *partners)


def far_call(reach, queries, state, partners, columns, scale):
    space, rows, feat = queries.shape
    return pl.pallas_call(
        functools.partial(far_kernel, space * rows, columns, scale),
        in_specs=[pl.BlockSpec(memory_space=pltpu.SMEM)]
        + [pl.BlockSpec(memory_space=pltpu.VMEM)] * (4 + len(columns)),
        out_specs=pl.BlockSpec(memory_space=pltpu.VMEM),
        out_shape=jax.ShapeDtypeStruct((space, rows, feat), jnp.bfloat16),
        compiler_params=pltpu.CompilerParams(vmem_limit_bytes=vmem_bytes),
        cost_estimate=pl.CostEstimate(
            flops=2_000_000_000, bytes_accessed=4_000_000, transcendentals=500_000
        ),
        name="far_and_merge",
    )(reach, queries, *state, *partners)


def heads_plan(queries, keys, values, windows, scale):
    rows, feat = queries.shape[1:]
    space = lax.axis_size("space")
    frame_pos = lax.axis_index("frame")
    frame_count = lax.axis_size("frame")
    wide = feat // space

    distance = 2 ** jnp.arange(OCTAVES, dtype=jnp.int32)
    below = jnp.where(frame_pos - distance >= 0, windows[0, 0::2], -1)
    above = jnp.where(frame_pos + distance < frame_count, windows[0, 1::2], -1)
    upper = ((frame_pos & 1) == 0) == (distance == 1)
    reach = jnp.concatenate([jnp.where(upper, above, below), jnp.where(upper, below, above)])

    pair = jnp.stack([keys[0], values[0]]).reshape(2, rows, space, wide)
    own = lax.all_to_all(jnp.transpose(pair, (2, 0, 1, 3)), "space", 0, 0, tiled=True)

    split = jnp.transpose(queries[0].reshape(rows, space, wide), (1, 0, 2))
    first_eight = crossed(own, 8, 1, lambda frame, length: True)
    first_two = crossed(own, 2, 1)
    second_two = crossed(own, 2, -1)
    first_one = crossed(own, 1, 1)
    split = lax.all_to_all(split, "space", 0, 0, tiled=True)
    first_two, second_two, split = lax.optimization_barrier((first_two, second_two, split))
    first_four = crossed(first_two, 2, 1)
    second_four = crossed(second_two, 2, -1)
    own_late, _ = lax.optimization_barrier((own, first_two))
    second_one = crossed(own_late, 1, -1)
    second_eight = crossed(first_eight, 16, -1, has_other_far)

    near = [first_one, first_two, second_two]
    state = near_call(reach, split, own, near, [0, 1, 5], scale)
    far = [second_one, first_four, second_four, first_eight, second_eight]
    result = far_call(reach, split, state, far, [4, 2, 6, 3, 7], scale)
    result = lax.all_to_all(result, "space", 0, 0, tiled=True)
    return jnp.transpose(result, (1, 0, 2)).reshape(1, rows, feat)


def shards(queries, keys, values, windows):
    scale = math.log2(math.e) / math.sqrt(HD)
    return heads_plan(queries, keys, values, windows, scale)


def solution(mesh):
    return jax.shard_map(
        shards,
        mesh=mesh,
        in_specs=(
            P("frame", "space", None),
            P("frame", "space", None),
            P("frame", "space", None),
            P("frame", None),
        ),
        out_specs=P("frame", "space", None),
        check_vma=False,
    )
```

```python
import functools
import math

import jax
import jax.numpy as jnp
from jax import lax
from jax.experimental import pallas as pl
from jax.experimental.pallas import tpu as pltpu
from jax.sharding import PartitionSpec as P

HD = 128
OCTAVES = 4
Q_ROWS = 64
K_ROWS = 128

neg_large = -1e30
vmem_bytes = 40 * 1024 * 1024


def crossed(array, by, sense, keep=None):
    length = lax.axis_size("frame")
    pairs = []
    for frame in range(length):
        target = frame + by * (sense if frame % 2 == 0 else -sense)
        if keep is None and 0 <= target < length:
            pairs.append((frame, target))
        elif keep is not None and keep(target % length, length):
            pairs.append((frame, target % length))
    return lax.ppermute(array, "frame", pairs)


def has_other_far(frame, length):
    return frame + 8 < length if frame % 2 == 0 else frame >= 8


def dot_nt(left, right):
    return lax.dot_general(
        left, right, (((1,), (1,)), ((), ())), preferred_element_type=jnp.float32
    )


def dot_nn(left, right):
    return lax.dot_general(
        left, right, (((1,), (0,)), ((), ())), preferred_element_type=jnp.float32
    )


def key_start(block, frame_rows):
    return min(max(block * Q_ROWS - (K_ROWS - Q_ROWS) // 2, 0), frame_rows - K_ROWS)


def rows_of(ref, part, at, start=0, count=None):
    whole = ref[:, part, :, at] if part is not None else ref[:, :, at]
    whole = whole.reshape(whole.shape[0] * whole.shape[1], HD)
    return whole if count is None else whole[start : start + count]


def banded(query_block, block, frame_rows, reach, refs, at, lean, scale):
    start = key_start(block, frame_rows)
    gap = jnp.abs(lean + (block * Q_ROWS - start))
    tiles = []
    for ref, limit in zip(refs, reach):
        keys = rows_of(ref, 0, at, start, K_ROWS)
        tiles.append(jnp.where(gap <= limit, dot_nt(query_block, keys) * scale, neg_large))
    return tiles


def folded(tiles, combine):
    while len(tiles) > 1:
        tiles = [
            combine(*tiles[i : i + 2]) if i + 1 < len(tiles) else tiles[i]
            for i in range(0, len(tiles), 2)
        ]
    return tiles[0]


def row_gap():
    return lax.broadcasted_iota(jnp.int32, (Q_ROWS, K_ROWS), 0) - lax.broadcasted_iota(
        jnp.int32, (Q_ROWS, K_ROWS), 1
    )


def weigh(tiles, top):
    weights = [jnp.exp2(tile - top) for tile in tiles]
    total = jnp.sum(folded(weights, jnp.add), axis=1, keepdims=True)
    return jnp.concatenate([w.astype(jnp.bfloat16) for w in weights], 1), total


def near_kernel(frame_rows, columns, scale, reach, queries, own, *refs):
    partner_refs = refs[: len(columns)]
    top_out, sum_out, product_out = refs[len(columns) :]
    lean = row_gap()
    limits = [reach[column] for column in columns]
    blocks = range(frame_rows // Q_ROWS)
    for head in range(queries.shape[2] // HD):
        at = slice(head * HD, (head + 1) * HD)
        all_queries = rows_of(queries, None, at)
        own_keys = rows_of(own, 0, at)
        own_values = rows_of(own, 1, at)
        for block in blocks:
            rows = slice(block * Q_ROWS, (block + 1) * Q_ROWS)
            query_block = all_queries[rows]
            own_scores = dot_nt(query_block, own_keys) * scale
            tiles = [own_scores[:, k : k + K_ROWS] for k in range(0, frame_rows, K_ROWS)]
            tiles += banded(
                query_block, block, frame_rows, limits, partner_refs, at, lean, scale
            )
            top = jnp.max(folded(tiles, jnp.maximum), axis=1, keepdims=True)
            weights, total = weigh(tiles, top)
            start = key_start(block, frame_rows)
            values = [rows_of(ref, 1, at, start, K_ROWS) for ref in partner_refs]
            top_out[head, rows] = jnp.broadcast_to(top, (Q_ROWS, HD))
            sum_out[head, rows] = jnp.broadcast_to(total, (Q_ROWS, HD))
            product_out[head, rows] = dot_nn(weights, jnp.concatenate([own_values] + values, 0))


def far_kernel(frame_rows, columns, scale, reach, queries, top_in, sum_in, product_in, *refs):
    partner_refs = refs[: len(columns)]
    out = refs[len(columns)]
    lean = row_gap()
    limits = [reach[column] for column in columns]
    parts = Q_ROWS // out.shape[1]
    blocks = range(frame_rows // Q_ROWS)
    span = [slice(block * Q_ROWS, (block + 1) * Q_ROWS) for block in blocks]
    for head in range(queries.shape[2] // HD):
        at = slice(head * HD, (head + 1) * HD)
        all_queries = rows_of(queries, None, at)
        tiles = [
            banded(all_queries[span[b]], b, frame_rows, limits, partner_refs, at, lean, scale)
            for b in blocks
        ]
        tops = [
            jnp.maximum(
                top_in[head, span[b]],
                jnp.max(folded(tiles[b], jnp.maximum), axis=1, keepdims=True),
            )
            for b in blocks
        ]
        weighed = [weigh(tiles[b], tops[b]) for b in blocks]
        products = [
            dot_nn(
                weighed[b][0],
                jnp.concatenate(
                    [
                        rows_of(ref, 1, at, key_start(b, frame_rows), K_ROWS)
                        for ref in partner_refs
                    ],
                    0,
                ),
            )
            for b in blocks
        ]
        for b in blocks:
            shrink = jnp.exp2(top_in[head, span[b]] - tops[b])
            total = sum_in[head, span[b]] * shrink + weighed[b][1]
            product = product_in[head, span[b]] * shrink + products[b]
            out[b * parts : (b + 1) * parts, :, at] = (
                (product / total).astype(jnp.bfloat16).reshape(parts, out.shape[1], HD)
            )


def near_call(reach, queries, own, partners, columns, scale):
    space, rows, feat = queries.shape
    state = jax.ShapeDtypeStruct((feat // HD, space * rows, HD), jnp.float32)
    return pl.pallas_call(
        functools.partial(near_kernel, space * rows, columns, scale),
        in_specs=[pl.BlockSpec(memory_space=pltpu.SMEM)]
        + [pl.BlockSpec(memory_space=pltpu.VMEM)] * (2 + len(columns)),
        out_specs=[pl.BlockSpec(memory_space=pltpu.VMEM)] * 3,
        out_shape=[state] * 3,
        compiler_params=pltpu.CompilerParams(vmem_limit_bytes=vmem_bytes),
        cost_estimate=pl.CostEstimate(
            flops=1_000_000_000, bytes_accessed=6_000_000, transcendentals=1_000_000
        ),
        name="own_and_near",
    )(reach, queries, own, *partners)


def far_call(reach, queries, state, partners, columns, scale):
    space, rows, feat = queries.shape
    return pl.pallas_call(
        functools.partial(far_kernel, space * rows, columns, scale),
        in_specs=[pl.BlockSpec(memory_space=pltpu.SMEM)]
        + [pl.BlockSpec(memory_space=pltpu.VMEM)] * (4 + len(columns)),
        out_specs=pl.BlockSpec(memory_space=pltpu.VMEM),
        out_shape=jax.ShapeDtypeStruct((space, rows, feat), jnp.bfloat16),
        compiler_params=pltpu.CompilerParams(vmem_limit_bytes=vmem_bytes),
        cost_estimate=pl.CostEstimate(
            flops=2_000_000_000, bytes_accessed=4_000_000, transcendentals=500_000
        ),
        name="far_and_merge",
    )(reach, queries, *state, *partners)


def heads_plan(queries, keys, values, windows, scale):
    rows, feat = queries.shape[1:]
    space = lax.axis_size("space")
    frame_pos = lax.axis_index("frame")
    frame_count = lax.axis_size("frame")
    wide = feat // space

    distance = 2 ** jnp.arange(OCTAVES, dtype=jnp.int32)
    below = jnp.where(frame_pos - distance >= 0, windows[0, 0::2], -1)
    above = jnp.where(frame_pos + distance < frame_count, windows[0, 1::2], -1)
    upper = ((frame_pos & 1) == 0) == (distance == 1)
    reach = jnp.concatenate([jnp.where(upper, above, below), jnp.where(upper, below, above)])

    pair = jnp.stack([keys[0], values[0]]).reshape(2, rows, space, wide)
    own = lax.all_to_all(jnp.transpose(pair, (2, 0, 1, 3)), "space", 0, 0, tiled=True)

    split = jnp.transpose(queries[0].reshape(rows, space, wide), (1, 0, 2))
    first_eight = crossed(own, 8, 1, lambda frame, length: True)
    first_two = crossed(own, 2, 1)
    second_two = crossed(own, 2, -1)
    first_one = crossed(own, 1, 1)
    split = lax.all_to_all(split, "space", 0, 0, tiled=True)
    first_two, second_two, split = lax.optimization_barrier((first_two, second_two, split))
    first_four = crossed(first_two, 2, 1)
    second_two_late, first_eight = lax.optimization_barrier((second_two, first_eight))
    second_four = crossed(second_two_late, 2, -1)
    own_late, _ = lax.optimization_barrier((own, first_two))
    second_one = crossed(own_late, 1, -1)
    second_eight = crossed(first_eight, 16, -1, has_other_far)

    near = [first_one, first_two, second_two]
    state = near_call(reach, split, own, near, [0, 1, 5], scale)
    far = [second_one, first_four, second_four, first_eight, second_eight]
    result = far_call(reach, split, state, far, [4, 2, 6, 3, 7], scale)
    result = lax.all_to_all(result, "space", 0, 0, tiled=True)
    return jnp.transpose(result, (1, 0, 2)).reshape(1, rows, feat)


def shards(queries, keys, values, windows):
    scale = math.log2(math.e) / math.sqrt(HD)
    return heads_plan(queries, keys, values, windows, scale)


def solution(mesh):
    return jax.shard_map(
        shards,
        mesh=mesh,
        in_specs=(
            P("frame", "space", None),
            P("frame", "space", None),
            P("frame", "space", None),
            P("frame", None),
        ),
        out_specs=P("frame", "space", None),
        check_vma=False,
    )
```
